32 devices in a mesh: rep: 8 (over y, x, core), shard: 4 (over z).
Axes of the slice: x: 2, y: 2, z: 4, core: 2. Of those that a mesh axis runs over, the one named last changes fastest.
Arguments:
- tokens: bfloat16 [32768, 1024], P(('rep', 'shard')), may hold values from -6 to 6
- segments: int32 [32, 1024], P(('rep', 'shard')), may hold values from 0 to 3, never falling along the last dimension, each value on 1 to 768 neighbouring positions
- ln1_gain: bfloat16 [1024], P('shard'), may hold values from 0.099609375 to 1.8984375
- ln1_bias: bfloat16 [1024], P('shard'), may hold values from -3 to 3
- w_qkv: bfloat16 [1024, 3072], P('shard'), may hold values from -0.1875 to 0.1875
- q_bias: bfloat16 [1024], P('shard'), may hold values from -3 to 3
- v_bias: bfloat16 [1024], P('shard'), may hold values from -3 to 3
- w_out: bfloat16 [1024, 1024], P('shard'), may hold values from -0.5 to 0.5
- out_bias: bfloat16 [1024], P('shard'), may hold values from -3 to 3
- ln2_gain: bfloat16 [1024], P('shard'), may hold values from 0.099609375 to 1.8984375
- ln2_bias: bfloat16 [1024], P('shard'), may hold values from -3 to 3
- w_up: bfloat16 [1024, 4096], P('shard'), may hold values from -0.1875 to 0.1875
- up_bias: bfloat16 [4096], P('shard'), may hold values from -3 to 3
- w_down: bfloat16 [4096, 1024], P('shard'), may hold values from -0.09375 to 0.09375
- down_bias: bfloat16 [1024], P('shard'), may hold values from -3 to 3
- cotangent: bfloat16 [32768, 1024], P(('rep', 'shard')), may hold values from -6 to 6
Outputs:
- output: bfloat16 [32768, 1024], P(('rep', 'shard'))
- token_grad: bfloat16 [32768, 1024], P(('rep', 'shard'))
- ln1_gain_grad: float32 [1024], P('shard')
- ln1_bias_grad: float32 [1024], P('shard')
- w_qkv_grad: float32 [1024, 3072], P('shard')
- q_bias_grad: float32 [1024], P('shard')
- v_bias_grad: float32 [1024], P('shard')
- w_out_grad: float32 [1024, 1024], P('shard')
- out_bias_grad: float32 [1024], P('shard')
- ln2_gain_grad: float32 [1024], P('shard')
- ln2_bias_grad: float32 [1024], P('shard')
- w_up_grad: float32 [1024, 4096], P('shard')
- up_bias_grad: float32 [4096], P('shard')
- w_down_grad: float32 [4096, 1024], P('shard')
- down_bias_grad: float32 [1024], P('shard')
The draws below stay inside these ranges and needn't reach their ends.
Inputs may be any that keep to these rules, and one draw needn't show every extreme that they name: `segments`: within each sequence the numbers start at 0, never fall and name every document 0 to 3; each document has at most 768 tokens and one has exactly 768.
All inputs are finite; a program needn't handle non-finite values.
Results may differ from the reference program's by a relative error of at most 0.014.
Values may be sent and summed in bfloat16 or wider, within the bound.
A program may use at most 320 MiB of HBM per device.

```python
import math
import jax
import jax.numpy as jnp
import numpy as np
from jax import lax

D = 1024
HEADS = 16
FF = 4096
TOK_DEV = 1024
HEAD_DIM = 64
SEQS = 32
TOKENS = 32768
DOCS = 4
DOC_MOST = 768


def steps_of(key, shape, shards, low, top_value):
    def one(axis_at, shards_of):
        steps = jax.random.uniform(jax.random.fold_in(jax.random.fold_in(key, 6), axis_at), (shards_of,), jnp.float32, low / len(shards), top_value / len(shards))
        return jnp.repeat(jnp.exp(steps), shape[axis_at] // shards_of).reshape((-1,) + (1,) * (len(shape) - axis_at - 1))

    loudness = one(*shards[0])
    for cut in shards[1:]:
        loudness = loudness * one(*cut)
    return loudness


def length_profile(count, total, bound, slope):
    portions = [(1 << 20) // math.isqrt(standing ** slope) + 1 for standing in range(2, count + 1)]
    surplus, given = total - bound - (count - 1), [1] * (count - 1)
    while surplus > 0:
        free = [i for i in range(count - 1) if given[i] < bound]
        mass, left = sum([portions[i] for i in free]), surplus
        for i in free:
            more = min(bound - given[i], max(1, left * portions[i] // mass), surplus)
            given[i] = given[i] + more
            surplus = surplus - more
    return np.array([bound] + given)


def uneven(rng, amount, total, most, slope):
    if amount == 2:
        one = jax.random.randint(rng, (), max(1, total - most), min(most, total - 1) + 1)
        return jnp.stack([one, total - one])
    lengths = jnp.asarray(length_profile(amount, total, most, slope), jnp.int32)
    couples = (amount - 1) // 2
    donor, receiver = lengths[1:1 + 2 * couples:2], lengths[2:2 + 2 * couples:2]
    slack = jnp.minimum(donor - 1, most - receiver)
    passed = jax.random.randint(jax.random.fold_in(rng, 1), (couples,), 0, 1 << 20) % (slack + 1)
    lengths = lengths.at[1:1 + 2 * couples:2].set(donor - passed).at[2:2 + 2 * couples:2].set(receiver + passed)
    return lengths[jax.random.permutation(jax.random.fold_in(rng, 2), amount)]


def bell_draw(own_key, extent, scale, reach, cuts=(), kind=jnp.bfloat16):
    level = steps_of(own_key, extent, cuts, -0.22, 0.18) if cuts else 1.0
    array = jax.random.normal(own_key, extent, jnp.float32) * scale * level
    return jnp.minimum(jnp.maximum(array, -reach), reach).astype(kind)


def setup_inputs(seed: int = 0) -> dict:
    streams_of = jax.random.split(jax.random.key(seed), 17)
    return {
        "tokens": bell_draw(streams_of[0], (TOKENS, D), 1.0, 6.0, ((0, 32),)),
        "segments": jax.vmap(lambda own: jnp.searchsorted(jnp.cumsum(uneven(own, DOCS, TOK_DEV, DOC_MOST, 2)), jnp.arange(TOK_DEV), side="right"))(jax.random.split(streams_of[1], SEQS)).reshape((SEQS, TOK_DEV)).astype(jnp.int32),
        "ln1_gain": jnp.clip(1.0 + 0.18 * jax.random.normal(streams_of[2], (D,), jnp.float32), 0.099609375, 1.8984375).astype(jnp.bfloat16),
        "ln1_bias": bell_draw(streams_of[3], (D,), 0.5, 3.0, ((0, 4),)),
        "w_qkv": bell_draw(streams_of[4], (D, 3 * D), D ** -0.5, 0.1875, ((0, 4),)),
        "q_bias": bell_draw(streams_of[5], (D,), 0.5, 3.0, ((0, 4),)),
        "v_bias": bell_draw(streams_of[6], (D,), 0.5, 3.0, ((0, 4),)),
        "w_out": bell_draw(streams_of[7], (D, D), (D // 8) ** -0.5, 0.5, ((0, 4),)),
        "out_bias": bell_draw(streams_of[8], (D,), 0.5, 3.0, ((0, 4),)),
        "ln2_gain": jnp.clip(1.0 + 0.18 * jax.random.normal(streams_of[9], (D,), jnp.float32), 0.099609375, 1.8984375).astype(jnp.bfloat16),
        "ln2_bias": bell_draw(streams_of[10], (D,), 0.5, 3.0, ((0, 4),)),
        "w_up": bell_draw(streams_of[11], (D, FF), D ** -0.5, 0.1875, ((0, 4),)),
        "up_bias": bell_draw(streams_of[12], (FF,), 0.5, 3.0, ((0, 4),)),
        "w_down": bell_draw(streams_of[13], (FF, D), FF ** -0.5, 0.09375, ((0, 4),)),
        "down_bias": bell_draw(streams_of[14], (D,), 0.5, 3.0, ((0, 4),)),
        "cotangent": bell_draw(streams_of[15], (TOKENS, D), 1.0, 6.0, ((0, 32),)),
    }


EPS = 1e-05
GELU_C = 0.7978845608028654
GELU_A = 0.044715

@jax.custom_vjp
def low(v):
    return lax.optimization_barrier(v.astype(jnp.bfloat16)).astype(jnp.float32)

@jax.custom_vjp
def low_back(v):
    return v

def low_keep(v):
    return (low(v), None)

def low_pass(kept, grad):
    return (grad,)

def back_keep(v):
    return (v, None)

def back_low(kept, grad):
    return (low(grad),)
low.defvjp(low_keep, low_pass)
low_back.defvjp(back_keep, back_low)

def matmul(left, right):
    return jnp.dot(left, right, precision=lax.Precision.HIGHEST, preferred_element_type=jnp.float32)

def layer_norm(values, gain, shift):
    centred = values - lax.optimization_barrier(jnp.mean(values, axis=-1, keepdims=True))
    scale = lax.rsqrt(lax.optimization_barrier(jnp.mean(centred * centred, axis=-1, keepdims=True)) + EPS)
    return centred * scale * gain + shift

def gelu_tanh(values):
    return 0.5 * values * (1.0 + jnp.tanh(GELU_C * (values + GELU_A * values * values * values)))

def forward(inputs, params, seg):
    gain_one, shift_one, qkv_matrix, query_bias, value_bias, out_matrix, out_shift, gain_two, shift_two, up_matrix, up_shift, down_matrix, down_shift = params
    rows = inputs.shape[0]
    block = min(512, rows)
    count = rows // block
    first = low(layer_norm(inputs, gain_one, shift_one))
    joined = jnp.concatenate([query_bias, jnp.zeros_like(query_bias), value_bias])
    qkv = low(low_back(matmul(first, qkv_matrix) + joined))
    query = qkv[:, :D].reshape(rows, HEADS, HEAD_DIM)
    keys = qkv[:, D:2 * D].reshape(rows, HEADS, HEAD_DIM)
    values = qkv[:, 2 * D:].reshape(rows, HEADS, HEAD_DIM)
    slopes = 2.0 ** (-8.0 * (jnp.arange(HEADS, dtype=jnp.float32) + 1.0) / HEADS)
    scale = HEAD_DIM ** (-0.5)
    key_pos = jnp.arange(rows, dtype=jnp.int32)

    def attend(item):
        q_blk, s_blk, start = item
        raw = jnp.einsum('qhd,khd->hqk', q_blk, keys, precision=lax.Precision.HIGHEST) * scale
        raw = low_back(raw)
        query_pos = start + jnp.arange(block, dtype=jnp.int32)
        dist = (key_pos[None, :] - query_pos[:, None]).astype(jnp.float32)
        scores = raw + slopes[:, None, None] * dist[None]
        allowed = (key_pos[None, :] <= query_pos[:, None]) & (s_blk[:, None] == seg[None, :])
        scores = jnp.where(allowed[None], scores, -1e+30)
        top = lax.optimization_barrier(jnp.max(scores, axis=-1, keepdims=True))
        weights = jnp.exp(scores - top)
        probs = weights / lax.optimization_barrier(jnp.sum(weights, axis=-1, keepdims=True))
        return jnp.einsum('hqk,khd->qhd', low(probs), values, precision=lax.Precision.HIGHEST)
    starts = jnp.arange(count, dtype=jnp.int32) * block
    mixed = lax.map(jax.checkpoint(attend), (query.reshape(count, block, HEADS, HEAD_DIM), seg.reshape(count, block), starts))
    mixed = low(low_back(mixed.reshape(rows, D)))
    middle = inputs + low_back(matmul(mixed, out_matrix) + out_shift)
    second = low(layer_norm(middle, gain_two, shift_two))
    upper = low_back(matmul(second, up_matrix) + up_shift)
    active = low(gelu_tanh(upper))
    return middle + low_back(matmul(active, down_matrix) + down_shift)

def reference(tokens, segments, ln1_gain, ln1_bias, w_qkv, q_bias, v_bias, w_out, out_bias, ln2_gain, ln2_bias, w_up, up_bias, w_down, down_bias, cotangent):
    params = tuple((p.astype(jnp.float32) for p in (ln1_gain, ln1_bias, w_qkv, q_bias, v_bias, w_out, out_bias, ln2_gain, ln2_bias, w_up, up_bias, w_down, down_bias)))
    seqs = segments.shape[0]
    token_seqs = tokens.astype(jnp.float32).reshape(seqs, TOK_DEV, D)
    cot_seqs = cotangent.astype(jnp.float32).reshape(seqs, TOK_DEV, D)

    def one(totals, item):
        inputs, seg, cot = item
        result, pull = jax.vjp(lambda v, p: forward(v, p, seg), inputs, params)
        grad_inputs, grad_params = pull(cot)
        totals = jax.tree.map(lambda a, b: a + b, totals, grad_params)
        return (totals, (result.astype(jnp.bfloat16), grad_inputs.astype(jnp.bfloat16)))
    init = jax.tree.map(jnp.zeros_like, params)
    totals, (results, grads) = lax.scan(one, init, (token_seqs, segments, cot_seqs))
    return (results.reshape(seqs * TOK_DEV, D), grads.reshape(seqs * TOK_DEV, D), totals[0], totals[1], totals[2], totals[3], totals[4], totals[5], totals[6], totals[7], totals[8], totals[9], totals[10], totals[11], totals[12])
```

```python
import functools

import jax
import jax.numpy as jnp
from jax import lax
from jax.experimental import pallas as pl
from jax.experimental.pallas import tpu as pltpu
from jax.sharding import PartitionSpec as P

HEADS = 16


EPS = 1e-05
GELU_C = 0.7978845608028654
GELU_A = 0.044715


def normalize(values):
    centred = values - jnp.mean(values, axis=-1, keepdims=True)
    scale = lax.rsqrt(jnp.mean(centred * centred, axis=-1, keepdims=True) + EPS)
    return (centred * scale, scale)


def norm_back(grad_h, normed, scale, gain):
    grad_n = grad_h * gain
    return scale * (
        grad_n
        - jnp.mean(grad_n, axis=-1, keepdims=True)
        - normed * jnp.mean(grad_n * normed, axis=-1, keepdims=True)
    )


def left_dot(left, right):
    return lax.dot_general(
        left, right, (((0,), (0,)), ((), ())), preferred_element_type=jnp.float32
    )


def right_dot(left, right):
    return lax.dot_general(
        left, right, (((1,), (1,)), ((), ())), preferred_element_type=jnp.float32
    )


def column_sum(values):
    return jnp.sum(values.astype(jnp.float32), axis=0)

GROUP = 8
MIB = 1 << 20


def peers():
    rep = lax.axis_index("rep")
    shard = lax.axis_index("shard")
    place = lax.rem(rep, GROUP)
    core = lax.rem(place, 2)
    east = lax.rem(place // 2, 2)
    north = place // 4
    return (
        rep,
        shard,
        (core, north, east),
        rep + 1 - 2 * core,
        rep + 2 - 4 * east,
        rep + 4 - 8 * north,
    )


def greet(count):
    rep, shard, _, core_peer, x_peer, y_peer = peers()
    barrier = pltpu.get_barrier_semaphore()
    for peer in (core_peer, x_peer, y_peer):
        pl.semaphore_signal(
            barrier, inc=1, device_id=(peer, shard), device_id_type=pl.DeviceIdType.MESH
        )
    for hop in range(1, count):
        pl.semaphore_signal(
            barrier,
            inc=1,
            device_id=(rep, lax.rem(shard + hop, count)),
            device_id_type=pl.DeviceIdType.MESH,
        )
    pl.semaphore_wait(barrier, 3 + count - 1)


def remote(source, target, send, recv, device):
    return pltpu.make_async_remote_copy(
        src_ref=source,
        dst_ref=target,
        send_sem=send,
        recv_sem=recv,
        device_id=device,
        device_id_type=pl.DeviceIdType.MESH,
    )


def gather_kernel(count, number, *refs):
    ins, outs = refs[:number], refs[number : 2 * number]
    send, recv, local = refs[2 * number :]
    rep, shard, (c, y, x), core_peer, x_peer, y_peer = peers()
    greet(count)
    started = {}
    owns = []
    hops = range(1, count)

    def owner(hop):
        return lax.rem(shard + count - hop, count)

    def push(m, stage, hop, source, target, device):
        copy = remote(
            source, target, send.at[m, stage, hop - 1], recv.at[m, stage, hop - 1], device
        )
        copy.start()
        started[m, stage, hop] = copy

    def step(m, stage):
        out = outs[m]
        half = out.shape[-1] // 2
        low, high = pl.ds(0, half), pl.ds(half, half)
        if stage == 0:
            for hop in hops:
                push(
                    m,
                    0,
                    hop,
                    ins[m].at[c, y, x],
                    out.at[shard, c, y, x],
                    (rep, lax.rem(shard + hop, count)),
                )
            own = pltpu.make_async_copy(ins[m], out.at[shard], local.at[m])
            own.start()
            owns.append(own)
        elif stage == 1:
            for hop in hops:
                started[m, 0, hop].wait_recv()
                s = owner(hop)
                first = out.at[s, c, y, x, :, low]
                second = out.at[s, c, y, x, :, high]
                push(m, 1, hop, first, first, (x_peer, shard))
                push(m, 2, hop, second, second, (y_peer, shard))
        elif stage == 2:
            for hop in hops:
                s = owner(hop)
                started[m, 1, hop].wait_recv()
                first = out.at[s, c, y, :, :, low]
                push(m, 3, hop, first, first, (y_peer, shard))
                started[m, 2, hop].wait_recv()
                second = out.at[s, c, :, x, :, high]
                push(m, 4, hop, second, second, (x_peer, shard))
        elif stage == 3:
            for hop in hops:
                s = owner(hop)
                started[m, 3, hop].wait_recv()
                started[m, 4, hop].wait_recv()
                push(m, 5, hop, out.at[s, c], out.at[s, c], (core_peer, shard))
        else:
            for hop in hops:
                started[m, 5, hop].wait_recv()

    for time in range(number + 4):
        for m in range(number):
            if 0 <= time - m <= 4:
                step(m, time - m)
    for copy in started.values():
        copy.wait_send()
    for own in owns:
        own.wait()


def gather_all(count, arrays):
    number = len(arrays)
    split = [a.reshape(2, 2, 2, a.shape[0] // GROUP, a.shape[1]) for a in arrays]
    outs = pl.pallas_call(
        functools.partial(gather_kernel, count, number),
        out_shape=[jax.ShapeDtypeStruct((count,) + a.shape, a.dtype) for a in split],
        in_specs=[pl.BlockSpec(memory_space=pl.ANY)] * number,
        out_specs=[pl.BlockSpec(memory_space=pl.ANY)] * number,
        scratch_shapes=[
            pltpu.SemaphoreType.DMA((number, 6, count - 1)),
            pltpu.SemaphoreType.DMA((number, 6, count - 1)),
            pltpu.SemaphoreType.DMA((number,)),
        ],
        compiler_params=pltpu.CompilerParams(
            collective_id=0, has_side_effects=True, vmem_limit_bytes=4 * MIB
        ),
        name="gather_parameters",
    )(*split)
    return [o.reshape(count * a.shape[0], a.shape[1]) for o, a in zip(outs, arrays)]


def add_into(target, source, lead, rows):
    chunk = 16

    def body(i, carry):
        at, sl = i // (rows // chunk), lax.rem(i, rows // chunk) * chunk
        sl = pl.ds(pl.multiple_of(sl, chunk), chunk)
        ref, index = target(at, sl)
        other, place = source(at, sl)
        ref[index] = (ref[index].astype(jnp.float32) + other[place].astype(jnp.float32)).astype(
            jnp.bfloat16
        )
        return carry

    lax.fori_loop(0, lead * (rows // chunk), body, 0)


def reduce_kernel(count, number, *refs):
    ins, outs = refs[:number], refs[number : 2 * number]
    scratch = refs[2 * number :]
    per = [scratch[7 * m : 7 * m + 7] for m in range(number)]
    send, recv, local = scratch[7 * number :]
    rep, shard, (c, y, x), core_peer, x_peer, y_peer = peers()
    greet(count)
    started = {}

    def push(m, k, source, target, device):
        copy = remote(source, target, send.at[m, k], recv.at[m, k], device)
        copy.start()
        started[m, k] = copy

    def step(m, stage):
        acc, r1, r2a, r2b, r3a, r3b, r4 = per[m]
        out = outs[m]
        rows, cols = acc.shape[-2:]
        half = cols // 2
        low, high = pl.ds(0, half), pl.ds(half, half)
        if stage == 0:
            push(m, 0, ins[m].at[:, 1 - c], r1, (core_peer, shard))
            own = pltpu.make_async_copy(ins[m].at[:, c], acc, local.at[m, 0])
            own.start()
            started[m, "own"] = own
        elif stage == 1:
            started[m, "own"].wait()
            started[m, 0].wait_recv()
            add_into(
                lambda i, sl: (acc, (i // 4, lax.rem(i // 2, 2), lax.rem(i, 2), sl)),
                lambda i, sl: (r1, (i // 4, lax.rem(i // 2, 2), lax.rem(i, 2), sl)),
                4 * count,
                rows,
            )
            push(m, 1, acc.at[:, 1 - y, :, :, low], r2a, (y_peer, shard))
            push(m, 2, acc.at[:, :, 1 - x, :, high], r2b, (x_peer, shard))
        elif stage == 2:
            started[m, 1].wait_recv()
            add_into(
                lambda i, sl: (acc, (i // 2, y, lax.rem(i, 2), sl, low)),
                lambda i, sl: (r2a, (i // 2, lax.rem(i, 2), sl)),
                2 * count,
                rows,
            )
            push(m, 3, acc.at[:, y, 1 - x, :, low], r3a, (x_peer, shard))
            started[m, 2].wait_recv()
            add_into(
                lambda i, sl: (acc, (i // 2, lax.rem(i, 2), x, sl, high)),
                lambda i, sl: (r2b, (i // 2, lax.rem(i, 2), sl)),
                2 * count,
                rows,
            )
            push(m, 4, acc.at[:, 1 - y, x, :, high], r3b, (y_peer, shard))
        elif stage == 3:
            started[m, 3].wait_recv()
            add_into(
                lambda i, sl: (acc, (i, y, x, sl, low)), lambda i, sl: (r3a, (i, sl)), count, rows
            )
            started[m, 4].wait_recv()
            add_into(
                lambda i, sl: (acc, (i, y, x, sl, high)), lambda i, sl: (r3b, (i, sl)), count, rows
            )
            for hop in range(1, count):
                to = lax.rem(shard + hop, count)
                push(m, 4 + hop, acc.at[to, y, x], r4.at[hop - 1], (rep, to))
        elif stage == 4:
            for hop in range(1, count):
                started[m, 4 + hop].wait_recv()

            def total(i, carry):
                sl = pl.ds(pl.multiple_of(i * 16, 16), 16)
                value = acc[shard, y, x, sl].astype(jnp.float32)
                for hop in range(1, count):
                    value = value + r4[hop - 1, sl].astype(jnp.float32)
                acc[shard, y, x, sl] = value.astype(jnp.bfloat16)
                return carry

            lax.fori_loop(0, rows // 16, total, 0)
            own = pltpu.make_async_copy(acc.at[shard, y, x], out.at[c, y, x], local.at[m, 1])
            own.start()
            started[m, "res"] = own
            k = 4 + count
            push(
                m, k, acc.at[shard, y, x, :, low], out.at[c, y, x, :, low], (x_peer, shard)
            )
            push(
                m, k + 1, acc.at[shard, y, x, :, high], out.at[c, y, x, :, high], (y_peer, shard)
            )
        elif stage == 5:
            k = 4 + count
            started[m, "res"].wait()
            started[m, k].wait_recv()
            first = out.at[c, y, :, :, low]
            push(m, k + 2, first, first, (y_peer, shard))
            started[m, k + 1].wait_recv()
            second = out.at[c, :, x, :, high]
            push(m, k + 3, second, second, (x_peer, shard))
        elif stage == 6:
            k = 4 + count
            started[m, k + 2].wait_recv()
            started[m, k + 3].wait_recv()
            push(m, k + 4, out.at[c], out.at[c], (core_peer, shard))
        else:
            started[m, 8 + count].wait_recv()

    for time in range(number + 7):
        for m in range(number):
            if 0 <= time - m <= 7:
                step(m, time - m)
    for (_, k), copy in started.items():
        if k not in ("own", "res"):
            copy.wait_send()


def reduce_all(count, arrays):
    number = len(arrays)
    split, scratch = [], []
    for a in arrays:
        rows, cols = a.shape[0] // (count * GROUP), a.shape[1]
        half = cols // 2
        split.append(a.reshape(count, 2, 2, 2, rows, cols))
        for shape in (
            (count, 2, 2, rows, cols),
            (count, 2, 2, rows, cols),
            (count, 2, rows, half),
            (count, 2, rows, half),
            (count, rows, half),
            (count, rows, half),
            (count - 1, rows, cols),
        ):
            scratch.append(pltpu.VMEM(shape, jnp.bfloat16))
    outs = pl.pallas_call(
        functools.partial(reduce_kernel, count, number),
        out_shape=[jax.ShapeDtypeStruct(a.shape[1:], a.dtype) for a in split],
        in_specs=[pl.BlockSpec(memory_space=pl.ANY)] * number,
        out_specs=[pl.BlockSpec(memory_space=pl.ANY)] * number,
        scratch_shapes=scratch
        + [
            pltpu.SemaphoreType.DMA((number, 9 + count)),
            pltpu.SemaphoreType.DMA((number, 9 + count)),
            pltpu.SemaphoreType.DMA((number, 2)),
        ],
        compiler_params=pltpu.CompilerParams(
            collective_id=1, has_side_effects=True, vmem_limit_bytes=48 * MIB
        ),
        name="reduce_gradients",
    )(*split)
    return [o.reshape(a.shape[0] // count, a.shape[1]) for o, a in zip(outs, arrays)]


def slope_of(heads, head):
    return jnp.exp2(jnp.full((1, 1), -8.0 / heads, jnp.float32) * (head + 1).astype(jnp.float32))


def set_distance(dist_ref, seg_row, seg_col):
    rows = dist_ref.shape[0]
    for start in range(0, rows, BLOCK):
        shape = (rows, BLOCK)
        key = lax.broadcasted_iota(jnp.int32, shape, 0)
        query = lax.broadcasted_iota(jnp.int32, shape, 1) + start
        allowed = (key <= query) & (seg_col[...] == seg_row[:, pl.ds(start, BLOCK)])
        dist_ref[:, pl.ds(start, BLOCK)] = jnp.where(
            allowed, (key - query).astype(jnp.float32), -1e30
        )


BLOCK = 256


def own_half(values, side, axis):
    place = lax.broadcasted_iota(jnp.int32, values.shape, axis)
    mine = (place < 64) if side == 0 else (place >= 64)
    return jnp.where(mine, values, jnp.zeros_like(values))


def scores_of(q_half, keys, dist, slope):
    raw = lax.dot_general(
        keys, q_half, (((1,), (1,)), ((), ())), preferred_element_type=jnp.float32
    )
    return raw + slope * dist


def attend_kernel(heads, seg_row, seg_col, q_ref, k_ref, v_ref, mixed_ref, lse_ref, dist_ref):
    rows, width = q_ref.shape
    step = pl.program_id(0)

    @pl.when(step == 0)
    def _():
        set_distance(dist_ref, seg_row, seg_col)

    for start in range(0, rows, BLOCK):
        seen = start + BLOCK
        at = pl.ds(start, BLOCK)
        query = q_ref[at, :] * jnp.bfloat16(0.125)
        parts = []
        for side in range(2):
            slope = slope_of(heads, step * 2 + side)
            scores = scores_of(
                own_half(query, side, 1), k_ref[0:seen, :], dist_ref[0:seen, at], slope
            )
            top = jnp.max(scores, axis=0, keepdims=True)
            weights = jnp.exp(scores - top)
            total = jnp.sum(weights, axis=0, keepdims=True)
            lse_ref[0, pl.ds(side, 1), at] = top + jnp.log(total)
            value = left_dot(v_ref[0:seen, :], weights.astype(jnp.bfloat16)) / total
            parts.append(value[side * 64 : side * 64 + 64])
        mixed_ref[at, :] = jnp.concatenate(parts, axis=0).T.astype(jnp.bfloat16)


def attend_back_kernel(
    heads,
    seg_row,
    seg_col,
    q_ref,
    k_ref,
    v_ref,
    gm_ref,
    lse_ref,
    gq_ref,
    gk_ref,
    gv_ref,
    dist_ref,
    sum_k,
    sum_v,
):
    rows, width = q_ref.shape
    step = pl.program_id(0)

    @pl.when(step == 0)
    def _():
        set_distance(dist_ref, seg_row, seg_col)

    for start in range(rows - BLOCK, -1, -BLOCK):
        seen = start + BLOCK
        at = pl.ds(start, BLOCK)
        query = q_ref[at, :] * jnp.bfloat16(0.125)
        grad = gm_ref[at, :]
        parts = []
        add_k = jnp.zeros((seen, width), jnp.float32)
        add_v = jnp.zeros((seen, width), jnp.float32)
        for side in range(2):
            slope = slope_of(heads, step * 2 + side)
            q_half = own_half(query, side, 1)
            g_half = own_half(grad, side, 1)
            scores = scores_of(q_half, k_ref[0:seen, :], dist_ref[0:seen, at], slope)
            probs = jnp.exp(scores - lse_ref[0, pl.ds(side, 1), at])
            grad_probs = right_dot(v_ref[0:seen, :], g_half)
            inner = jnp.sum(probs * grad_probs, axis=0, keepdims=True)
            grad_scores = (probs * (grad_probs - inner)).astype(jnp.bfloat16)
            value = left_dot(k_ref[0:seen, :], grad_scores) * 0.125
            parts.append(value[side * 64 : side * 64 + 64])
            add_k = add_k + jnp.dot(grad_scores, q_half, preferred_element_type=jnp.float32)
            add_v = add_v + jnp.dot(
                probs.astype(jnp.bfloat16), g_half, preferred_element_type=jnp.float32
            )
        gq_ref[at, :] = jnp.concatenate(parts, axis=0).T.astype(jnp.bfloat16)
        if seen == rows:
            sum_k[...] = add_k
            sum_v[...] = add_v
        else:
            sum_k[0:seen, :] += add_k
            sum_v[0:seen, :] += add_v
    gk_ref[...] = sum_k[...].astype(jnp.bfloat16)
    gv_ref[...] = sum_v[...].astype(jnp.bfloat16)


def attend(qkv, segments):
    rows, width = qkv.shape[0], qkv.shape[1] // 3
    pairs = width // 128
    return pl.pallas_call(
        functools.partial(attend_kernel, HEADS),
        grid=(pairs,),
        in_specs=[
            pl.BlockSpec((1, rows), lambda i: (0, 0)),
            pl.BlockSpec((rows, 1), lambda i: (0, 0)),
            pl.BlockSpec((rows, 128), lambda i: (0, i)),
            pl.BlockSpec((rows, 128), lambda i: (0, i + pairs)),
            pl.BlockSpec((rows, 128), lambda i: (0, i + 2 * pairs)),
        ],
        out_specs=[
            pl.BlockSpec((rows, 128), lambda i: (0, i)),
            pl.BlockSpec((1, 2, rows), lambda i: (i, 0, 0)),
        ],
        out_shape=[
            jax.ShapeDtypeStruct((rows, width), jnp.bfloat16),
            jax.ShapeDtypeStruct((pairs, 2, rows), jnp.float32),
        ],
        scratch_shapes=[pltpu.VMEM((rows, rows), jnp.float32)],
        compiler_params=pltpu.CompilerParams(vmem_limit_bytes=40 * MIB),
        name="attend",
    )(segments, segments.reshape(rows, 1), qkv, qkv, qkv)


def attend_back(qkv, segments, grad_mixed, lse):
    rows, width = grad_mixed.shape
    pairs = width // 128
    block = pl.BlockSpec((rows, 128), lambda i: (0, i))
    return pl.pallas_call(
        functools.partial(attend_back_kernel, HEADS),
        grid=(pairs,),
        in_specs=[
            pl.BlockSpec((1, rows), lambda i: (0, 0)),
            pl.BlockSpec((rows, 1), lambda i: (0, 0)),
            block,
            pl.BlockSpec((rows, 128), lambda i: (0, i + pairs)),
            pl.BlockSpec((rows, 128), lambda i: (0, i + 2 * pairs)),
            block,
            pl.BlockSpec((1, 2, rows), lambda i: (i, 0, 0)),
        ],
        out_specs=[block, block, block],
        out_shape=[jax.ShapeDtypeStruct((rows, width), jnp.bfloat16)] * 3,
        scratch_shapes=[
            pltpu.VMEM((rows, rows), jnp.float32),
            pltpu.VMEM((rows, 128), jnp.float32),
            pltpu.VMEM((rows, 128), jnp.float32),
        ],
        compiler_params=pltpu.CompilerParams(vmem_limit_bytes=40 * MIB),
        name="attend_back",
    )(segments, segments.reshape(rows, 1), qkv, qkv, qkv, grad_mixed, lse)


def pack(pieces, shape):
    joined = jnp.concatenate([p.astype(jnp.bfloat16) for p in pieces], axis=-1)
    room = shape[-2] * shape[-1] - joined.shape[-1]
    pad = [(0, 0)] * (joined.ndim - 1) + [(0, room)]
    return jnp.pad(joined, pad).reshape((-1, shape[-1]))


def unpack(packed, count, sizes):
    flat = packed.reshape(count, -1)
    out, at = [], 0
    for size in sizes:
        out.append(flat[:, at : at + size].reshape(-1))
        at += size
    return out


def shards(
    tokens,
    segments,
    ln1_gain,
    ln1_bias,
    w_qkv,
    q_bias,
    v_bias,
    w_out,
    out_bias,
    ln2_gain,
    ln2_bias,
    w_up,
    up_bias,
    w_down,
    down_bias,
    cotangent,
):
    count = lax.axis_size("shard")
    vectors = (
        ln1_gain,
        ln1_bias,
        q_bias,
        v_bias,
        out_bias,
        ln2_gain,
        ln2_bias,
        down_bias,
        up_bias,
    )
    sizes = [v.shape[0] for v in vectors]
    small_rows = -(-sum(sizes) // (256 * 128)) * 128
    small = (small_rows, 256)
    small_full, qkv_matrix, out_matrix, up_matrix, down_matrix = gather_all(
        count, [pack(vectors, small), w_qkv, w_out, w_up, w_down]
    )
    (
        first_gain,
        first_shift,
        query_bias,
        value_bias,
        out_shift,
        second_gain,
        second_shift,
        down_shift,
        up_shift,
    ) = unpack(small_full, count, sizes)
    rows, width = tokens.shape
    inputs = tokens.astype(jnp.float32)
    normed_one, scale_one = normalize(inputs)
    first = (normed_one * first_gain.astype(jnp.float32) + first_shift.astype(jnp.float32)).astype(
        jnp.bfloat16
    )
    joined = jnp.concatenate([query_bias, jnp.zeros_like(query_bias), value_bias]).astype(
        jnp.float32
    )
    qkv = (jnp.dot(first, qkv_matrix, preferred_element_type=jnp.float32) + joined).astype(
        jnp.bfloat16
    )
    mixed, lse = attend(qkv, segments)
    middle = (
        inputs
        + jnp.dot(mixed, out_matrix, preferred_element_type=jnp.float32)
        + out_shift.astype(jnp.float32)
    )
    normed_two, scale_two = normalize(middle)
    second = (
        normed_two * second_gain.astype(jnp.float32) + second_shift.astype(jnp.float32)
    ).astype(jnp.bfloat16)
    upper = jnp.dot(second, up_matrix, preferred_element_type=jnp.float32) + up_shift.astype(
        jnp.float32
    )
    tanh_value = jnp.tanh(GELU_C * (upper + GELU_A * upper * upper * upper))
    active = (0.5 * upper * (1.0 + tanh_value)).astype(jnp.bfloat16)
    output = (
        middle
        + jnp.dot(active, down_matrix, preferred_element_type=jnp.float32)
        + down_shift.astype(jnp.float32)
    ).astype(jnp.bfloat16)
    down_shift_grad = column_sum(cotangent)
    down_grad = left_dot(active, cotangent)
    grad_active = right_dot(cotangent, down_matrix)
    gelu_slope = 0.5 * (1.0 + tanh_value) + 0.5 * upper * (
        1.0 - tanh_value * tanh_value
    ) * GELU_C * (1.0 + 3.0 * GELU_A * upper * upper)
    grad_upper = (grad_active * gelu_slope).astype(jnp.bfloat16)
    up_shift_grad = column_sum(grad_upper)
    up_grad = left_dot(second, grad_upper)
    grad_second = right_dot(grad_upper, up_matrix)
    second_gain_grad = jnp.sum(grad_second * normed_two, axis=0)
    second_shift_grad = jnp.sum(grad_second, axis=0)
    grad_middle = cotangent.astype(jnp.float32) + norm_back(
        grad_second, normed_two, scale_two, second_gain.astype(jnp.float32)
    )
    grad_branch = grad_middle.astype(jnp.bfloat16)
    out_shift_grad = column_sum(grad_branch)
    out_grad = left_dot(mixed, grad_branch)
    grad_mixed = right_dot(grad_branch, out_matrix).astype(jnp.bfloat16)
    grad_qkv = jnp.concatenate(attend_back(qkv, segments, grad_mixed, lse), axis=1)
    query_bias_grad = column_sum(grad_qkv[:, :width])
    value_bias_grad = column_sum(grad_qkv[:, 2 * width :])
    qkv_grad = left_dot(first, grad_qkv)
    grad_first = right_dot(grad_qkv, qkv_matrix)
    first_gain_grad = jnp.sum(grad_first * normed_one, axis=0)
    first_shift_grad = jnp.sum(grad_first, axis=0)
    token_grad = (
        grad_middle + norm_back(grad_first, normed_one, scale_one, first_gain.astype(jnp.float32))
    ).astype(jnp.bfloat16)
    grads = (
        first_gain_grad,
        first_shift_grad,
        query_bias_grad,
        value_bias_grad,
        out_shift_grad,
        second_gain_grad,
        second_shift_grad,
        down_shift_grad,
        up_shift_grad,
    )
    packed = pack([g.reshape(count, -1) for g in grads], small)
    shares = reduce_all(
        count,
        [
            down_grad.astype(jnp.bfloat16),
            up_grad.astype(jnp.bfloat16),
            out_grad.astype(jnp.bfloat16),
            qkv_grad.astype(jnp.bfloat16),
            packed,
        ],
    )
    shares = [share.astype(jnp.float32) for share in shares]
    groups = lax.axis_size("rep") // GROUP
    if groups > 1:
        shares = [share / GROUP for share in lax.psum(shares, "rep")]
    down_sum, up_sum, out_sum, qkv_sum, small_sum = shares
    (
        ln1_gain_sum,
        ln1_bias_sum,
        q_bias_sum,
        v_bias_sum,
        out_bias_sum,
        ln2_gain_sum,
        ln2_bias_sum,
        down_bias_sum,
        up_bias_sum,
    ) = unpack(small_sum, 1, sizes)
    return (
        output,
        token_grad,
        ln1_gain_sum,
        ln1_bias_sum,
        qkv_sum,
        q_bias_sum,
        v_bias_sum,
        out_sum,
        out_bias_sum,
        ln2_gain_sum,
        ln2_bias_sum,
        up_sum,
        up_bias_sum,
        down_sum,
        down_bias_sum,
    )


def solution(mesh):
    in_specs = (
        P(("rep", "shard"), None),
        P(("rep", "shard"), None),
        P("shard"),
        P("shard"),
        P("shard", None),
        P("shard"),
        P("shard"),
        P("shard", None),
        P("shard"),
        P("shard"),
        P("shard"),
        P("shard", None),
        P("shard"),
        P("shard", None),
        P("shard"),
        P(("rep", "shard"), None),
    )
    out_specs = (
        P(("rep", "shard"), None),
        P(("rep", "shard"), None),
        P("shard"),
        P("shard"),
        P("shard", None),
        P("shard"),
        P("shard"),
        P("shard", None),
        P("shard"),
        P("shard"),
        P("shard"),
        P("shard", None),
        P("shard"),
        P("shard", None),
        P("shard"),
    )
    return jax.shard_map(shards, mesh=mesh, in_specs=in_specs, out_specs=out_specs, check_vma=False)
```

```python
import functools

import jax
import jax.numpy as jnp
from jax import lax
from jax.experimental import pallas as pl
from jax.experimental.layout import Layout, with_layout_constraint
from jax.experimental.pallas import tpu as pltpu
from jax.sharding import PartitionSpec as P

HEADS = 16


EPS = 1e-05
GELU_C = 0.7978845608028654
GELU_A = 0.044715


def normalize(values):
    centred = values - jnp.mean(values, axis=-1, keepdims=True)
    scale = lax.rsqrt(jnp.mean(centred * centred, axis=-1, keepdims=True) + EPS)
    return (centred * scale, scale)


def norm_back(grad_h, normed, scale, gain):
    grad_n = grad_h * gain
    return scale * (
        grad_n
        - jnp.mean(grad_n, axis=-1, keepdims=True)
        - normed * jnp.mean(grad_n * normed, axis=-1, keepdims=True)
    )


def left_dot(left, right):
    return lax.dot_general(
        left, right, (((0,), (0,)), ((), ())), preferred_element_type=jnp.float32
    )


def right_dot(left, right):
    return lax.dot_general(
        left, right, (((1,), (1,)), ((), ())), preferred_element_type=jnp.float32
    )


def by_rows(values):
    return with_layout_constraint(values, Layout((0, 1)))


def column_sum(values):
    return jnp.sum(values.astype(jnp.float32), axis=0)

GROUP = 8
MIB = 1 << 20


def peers():
    rep = lax.axis_index("rep")
    shard = lax.axis_index("shard")
    place = lax.rem(rep, GROUP)
    core = lax.rem(place, 2)
    east = lax.rem(place // 2, 2)
    north = place // 4
    return (
        rep,
        shard,
        (core, north, east),
        rep + 1 - 2 * core,
        rep + 2 - 4 * east,
        rep + 4 - 8 * north,
    )


def greet(count):
    rep, shard, _, core_peer, x_peer, y_peer = peers()
    barrier = pltpu.get_barrier_semaphore()
    for peer in (core_peer, x_peer, y_peer):
        pl.semaphore_signal(
            barrier, inc=1, device_id=(peer, shard), device_id_type=pl.DeviceIdType.MESH
        )
    for hop in range(1, count):
        pl.semaphore_signal(
            barrier,
            inc=1,
            device_id=(rep, lax.rem(shard + hop, count)),
            device_id_type=pl.DeviceIdType.MESH,
        )
    pl.semaphore_wait(barrier, 3 + count - 1)


CHUNK = 2 << 20


def cut(shapes):
    chunks = []
    for a, (rows, cols) in enumerate(shapes):
        parts = max(1, rows * cols // CHUNK)
        chunks += [(a, k * (cols // parts), cols // parts) for k in range(parts)]
    return chunks


def remote(source, target, send, recv, device):
    return pltpu.make_async_remote_copy(
        src_ref=source,
        dst_ref=target,
        send_sem=send,
        recv_sem=recv,
        device_id=device,
        device_id_type=pl.DeviceIdType.MESH,
    )


def gather_kernel(count, number, chunks, *refs):
    ins, outs = refs[:number], refs[number : 2 * number]
    send, recv, local = refs[2 * number :]
    rep, shard, (c, y, x), core_peer, x_peer, y_peer = peers()
    greet(count)
    started = {}
    owns = []
    hops = range(1, count)

    def owner(hop):
        return lax.rem(shard + count - hop, count)

    def push(m, stage, hop, source, target, device):
        copy = remote(
            source, target, send.at[m, stage, hop - 1], recv.at[m, stage, hop - 1], device
        )
        copy.start()
        started[m, stage, hop] = copy

    def step(m, stage):
        a, first_col, cols = chunks[m]
        out = outs[a]
        half = cols // 2
        every = pl.ds(first_col, cols)
        low, high = pl.ds(first_col, half), pl.ds(first_col + half, half)
        if stage == 0:
            for hop in hops:
                push(
                    m,
                    0,
                    hop,
                    ins[a].at[c, y, x, :, every],
                    out.at[shard, c, y, x, :, every],
                    (rep, lax.rem(shard + hop, count)),
                )
            if first_col == 0:
                own = pltpu.make_async_copy(ins[a], out.at[shard], local.at[a])
                own.start()
                owns.append(own)
        elif stage == 1:
            for hop in hops:
                started[m, 0, hop].wait_recv()
                s = owner(hop)
                first = out.at[s, c, y, x, :, low]
                second = out.at[s, c, y, x, :, high]
                push(m, 1, hop, first, first, (x_peer, shard))
                push(m, 2, hop, second, second, (y_peer, shard))
        elif stage == 2:
            for hop in hops:
                s = owner(hop)
                started[m, 1, hop].wait_recv()
                first = out.at[s, c, y, :, :, low]
                push(m, 3, hop, first, first, (y_peer, shard))
                started[m, 2, hop].wait_recv()
                second = out.at[s, c, :, x, :, high]
                push(m, 4, hop, second, second, (x_peer, shard))
        elif stage == 3:
            for hop in hops:
                s = owner(hop)
                started[m, 3, hop].wait_recv()
                started[m, 4, hop].wait_recv()
                done = out.at[s, c, :, :, :, every]
                push(m, 5, hop, done, done, (core_peer, shard))
        else:
            for hop in hops:
                started[m, 5, hop].wait_recv()

    for time in range(len(chunks) + 4):
        for m in range(len(chunks)):
            if 0 <= time - m <= 4:
                step(m, time - m)
    for copy in started.values():
        copy.wait_send()
    for own in owns:
        own.wait()


def gather_all(count, arrays):
    number = len(arrays)
    chunks = cut([(count * a.shape[0], a.shape[1]) for a in arrays])
    split = [a.reshape(2, 2, 2, a.shape[0] // GROUP, a.shape[1]) for a in arrays]
    outs = pl.pallas_call(
        functools.partial(gather_kernel, count, number, chunks),
        out_shape=[jax.ShapeDtypeStruct((count,) + a.shape, a.dtype) for a in split],
        in_specs=[pl.BlockSpec(memory_space=pl.ANY)] * number,
        out_specs=[pl.BlockSpec(memory_space=pl.ANY)] * number,
        scratch_shapes=[
            pltpu.SemaphoreType.DMA((len(chunks), 6, count - 1)),
            pltpu.SemaphoreType.DMA((len(chunks), 6, count - 1)),
            pltpu.SemaphoreType.DMA((number,)),
        ],
        compiler_params=pltpu.CompilerParams(
            collective_id=0, has_side_effects=True, vmem_limit_bytes=4 * MIB
        ),
        name="gather_parameters",
    )(*split)
    return [o.reshape(count * a.shape[0], a.shape[1]) for o, a in zip(outs, arrays)]


def add_into(target, source, lead, rows):
    chunk = 16

    def body(i, carry):
        at, sl = i // (rows // chunk), lax.rem(i, rows // chunk) * chunk
        sl = pl.ds(pl.multiple_of(sl, chunk), chunk)
        ref, index = target(at, sl)
        other, place = source(at, sl)
        ref[index] = (ref[index].astype(jnp.float32) + other[place].astype(jnp.float32)).astype(
            jnp.bfloat16
        )
        return carry

    lax.fori_loop(0, lead * (rows // chunk), body, 0)


def reduce_kernel(count, number, chunks, *refs):
    ins, outs = refs[:number], refs[number : 2 * number]
    scratch = refs[2 * number :]
    per = [scratch[7 * m : 7 * m + 7] for m in range(len(chunks))]
    send, recv, local = scratch[7 * len(chunks) :]
    rep, shard, (c, y, x), core_peer, x_peer, y_peer = peers()
    greet(count)
    started = {}

    def push(m, k, source, target, device):
        copy = remote(source, target, send.at[m, k], recv.at[m, k], device)
        copy.start()
        started[m, k] = copy

    def step(m, stage):
        acc, r1, r2a, r2b, r3a, r3b, r4 = per[m]
        a, first_col, cols = chunks[m]
        out = outs[a]
        rows = acc.shape[-2]
        half = cols // 2
        low, high = pl.ds(0, half), pl.ds(half, half)
        every = pl.ds(first_col, cols)
        out_low, out_high = pl.ds(first_col, half), pl.ds(first_col + half, half)
        if stage == 0:
            push(m, 0, ins[a].at[:, 1 - c, :, :, :, every], r1, (core_peer, shard))
            own = pltpu.make_async_copy(ins[a].at[:, c, :, :, :, every], acc, local.at[m, 0])
            own.start()
            started[m, "own"] = own
        elif stage == 1:
            started[m, "own"].wait()
            started[m, 0].wait_recv()
            add_into(
                lambda i, sl: (acc, (i // 4, lax.rem(i // 2, 2), lax.rem(i, 2), sl)),
                lambda i, sl: (r1, (i // 4, lax.rem(i // 2, 2), lax.rem(i, 2), sl)),
                4 * count,
                rows,
            )
            push(m, 1, acc.at[:, 1 - y, :, :, low], r2a, (y_peer, shard))
            push(m, 2, acc.at[:, :, 1 - x, :, high], r2b, (x_peer, shard))
        elif stage == 2:
            started[m, 1].wait_recv()
            add_into(
                lambda i, sl: (acc, (i // 2, y, lax.rem(i, 2), sl, low)),
                lambda i, sl: (r2a, (i // 2, lax.rem(i, 2), sl)),
                2 * count,
                rows,
            )
            push(m, 3, acc.at[:, y, 1 - x, :, low], r3a, (x_peer, shard))
            started[m, 2].wait_recv()
            add_into(
                lambda i, sl: (acc, (i // 2, lax.rem(i, 2), x, sl, high)),
                lambda i, sl: (r2b, (i // 2, lax.rem(i, 2), sl)),
                2 * count,
                rows,
            )
            push(m, 4, acc.at[:, 1 - y, x, :, high], r3b, (y_peer, shard))
        elif stage == 3:
            started[m, 3].wait_recv()
            add_into(
                lambda i, sl: (acc, (i, y, x, sl, low)), lambda i, sl: (r3a, (i, sl)), count, rows
            )
            started[m, 4].wait_recv()
            add_into(
                lambda i, sl: (acc, (i, y, x, sl, high)), lambda i, sl: (r3b, (i, sl)), count, rows
            )
            for hop in range(1, count):
                to = lax.rem(shard + hop, count)
                push(m, 4 + hop, acc.at[to, y, x], r4.at[hop - 1], (rep, to))
        elif stage == 4:
            for hop in range(1, count):
                started[m, 4 + hop].wait_recv()

            def total(i, carry):
                sl = pl.ds(pl.multiple_of(i * 16, 16), 16)
                value = acc[shard, y, x, sl].astype(jnp.float32)
                for hop in range(1, count):
                    value = value + r4[hop - 1, sl].astype(jnp.float32)
                acc[shard, y, x, sl] = value.astype(jnp.bfloat16)
                return carry

            lax.fori_loop(0, rows // 16, total, 0)
            own = pltpu.make_async_copy(
                acc.at[shard, y, x], out.at[c, y, x, :, every], local.at[m, 1]
            )
            own.start()
            started[m, "res"] = own
            k = 4 + count
            push(
                m, k, acc.at[shard, y, x, :, low], out.at[c, y, x, :, out_low], (x_peer, shard)
            )
            push(
                m, k + 1, acc.at[shard, y, x, :, high], out.at[c, y, x, :, out_high], (y_peer, shard)
            )
        elif stage == 5:
            k = 4 + count
            started[m, "res"].wait()
            started[m, k].wait_recv()
            first = out.at[c, y, :, :, out_low]
            push(m, k + 2, first, first, (y_peer, shard))
            started[m, k + 1].wait_recv()
            second = out.at[c, :, x, :, out_high]
            push(m, k + 3, second, second, (x_peer, shard))
        elif stage == 6:
            k = 4 + count
            started[m, k + 2].wait_recv()
            started[m, k + 3].wait_recv()
            done = out.at[c, :, :, :, every]
            push(m, k + 4, done, done, (core_peer, shard))
        else:
            started[m, 8 + count].wait_recv()

    for time in range(len(chunks) + 7):
        for m in range(len(chunks)):
            if 0 <= time - m <= 7:
                step(m, time - m)
    for (_, k), copy in started.items():
        if k not in ("own", "res"):
            copy.wait_send()


def reduce_all(count, arrays):
    number = len(arrays)
    chunks = cut([a.shape for a in arrays])
    split = [
        a.reshape(count, 2, 2, 2, a.shape[0] // (count * GROUP), a.shape[1]) for a in arrays
    ]
    scratch = []
    for a, _, cols in chunks:
        rows = split[a].shape[-2]
        half = cols // 2
        for shape in (
            (count, 2, 2, rows, cols),
            (count, 2, 2, rows, cols),
            (count, 2, rows, half),
            (count, 2, rows, half),
            (count, rows, half),
            (count, rows, half),
            (count - 1, rows, cols),
        ):
            scratch.append(pltpu.VMEM(shape, jnp.bfloat16))
    outs = pl.pallas_call(
        functools.partial(reduce_kernel, count, number, chunks),
        out_shape=[jax.ShapeDtypeStruct(a.shape[1:], a.dtype) for a in split],
        in_specs=[pl.BlockSpec(memory_space=pl.ANY)] * number,
        out_specs=[pl.BlockSpec(memory_space=pl.ANY)] * number,
        scratch_shapes=scratch
        + [
            pltpu.SemaphoreType.DMA((len(chunks), 9 + count)),
            pltpu.SemaphoreType.DMA((len(chunks), 9 + count)),
            pltpu.SemaphoreType.DMA((len(chunks), 2)),
        ],
        compiler_params=pltpu.CompilerParams(
            collective_id=1, has_side_effects=True, vmem_limit_bytes=48 * MIB
        ),
        name="reduce_gradients",
    )(*split)
    return [o.reshape(a.shape[0] // count, a.shape[1]) for o, a in zip(outs, arrays)]


def slope_of(heads, head):
    return jnp.exp2(jnp.full((1, 1), -8.0 / heads, jnp.float32) * (head + 1).astype(jnp.float32))


def set_distance(dist_ref, seg_row, seg_col):
    rows = dist_ref.shape[0]
    for start in range(0, rows, BLOCK):
        shape = (rows, BLOCK)
        key = lax.broadcasted_iota(jnp.int32, shape, 0)
        query = lax.broadcasted_iota(jnp.int32, shape, 1) + start
        allowed = (key <= query) & (seg_col[...] == seg_row[:, pl.ds(start, BLOCK)])
        dist_ref[:, pl.ds(start, BLOCK)] = jnp.where(
            allowed, (key - query).astype(jnp.float32), -1e30
        )


BLOCK = 256


def own_half(values, side, axis):
    place = lax.broadcasted_iota(jnp.int32, values.shape, axis)
    mine = (place < 64) if side == 0 else (place >= 64)
    return jnp.where(mine, values, jnp.zeros_like(values))


def scores_of(q_half, keys, dist, slope):
    raw = lax.dot_general(
        keys, q_half, (((1,), (1,)), ((), ())), preferred_element_type=jnp.float32
    )
    return raw + slope * dist


def attend_kernel(heads, seg_row, seg_col, q_ref, k_ref, v_ref, mixed_ref, lse_ref, dist_ref):
    rows, width = q_ref.shape
    step = pl.program_id(0)

    @pl.when(step == 0)
    def _():
        set_distance(dist_ref, seg_row, seg_col)

    for start in range(0, rows, BLOCK):
        seen = start + BLOCK
        at = pl.ds(start, BLOCK)
        query = q_ref[at, :] * jnp.bfloat16(0.125)
        parts = []
        for side in range(2):
            slope = slope_of(heads, step * 2 + side)
            scores = scores_of(
                own_half(query, side, 1), k_ref[0:seen, :], dist_ref[0:seen, at], slope
            )
            top = jnp.max(scores, axis=0, keepdims=True)
            weights = jnp.exp(scores - top)
            total = jnp.sum(weights, axis=0, keepdims=True)
            lse_ref[0, pl.ds(side, 1), at] = top + jnp.log(total)
            value = left_dot(v_ref[0:seen, :], weights.astype(jnp.bfloat16)) / total
            parts.append(value[side * 64 : side * 64 + 64])
        mixed_ref[at, :] = jnp.concatenate(parts, axis=0).T.astype(jnp.bfloat16)


def attend_back_kernel(
    heads,
    seg_row,
    seg_col,
    q_ref,
    k_ref,
    v_ref,
    gm_ref,
    lse_ref,
    gq_ref,
    gk_ref,
    gv_ref,
    dist_ref,
    sum_k,
    sum_v,
):
    rows, width = q_ref.shape
    step = pl.program_id(0)

    @pl.when(step == 0)
    def _():
        set_distance(dist_ref, seg_row, seg_col)

    for start in range(rows - BLOCK, -1, -BLOCK):
        seen = start + BLOCK
        at = pl.ds(start, BLOCK)
        query = q_ref[at, :] * jnp.bfloat16(0.125)
        grad = gm_ref[at, :]
        parts = []
        add_k = jnp.zeros((seen, width), jnp.float32)
        add_v = jnp.zeros((seen, width), jnp.float32)
        for side in range(2):
            slope = slope_of(heads, step * 2 + side)
            q_half = own_half(query, side, 1)
            g_half = own_half(grad, side, 1)
            scores = scores_of(q_half, k_ref[0:seen, :], dist_ref[0:seen, at], slope)
            probs = jnp.exp(scores - lse_ref[0, pl.ds(side, 1), at])
            grad_probs = right_dot(v_ref[0:seen, :], g_half)
            inner = jnp.sum(probs * grad_probs, axis=0, keepdims=True)
            grad_scores = (probs * (grad_probs - inner)).astype(jnp.bfloat16)
            value = left_dot(k_ref[0:seen, :], grad_scores) * 0.125
            parts.append(value[side * 64 : side * 64 + 64])
            add_k = add_k + jnp.dot(grad_scores, q_half, preferred_element_type=jnp.float32)
            add_v = add_v + jnp.dot(
                probs.astype(jnp.bfloat16), g_half, preferred_element_type=jnp.float32
            )
        gq_ref[at, :] = jnp.concatenate(parts, axis=0).T.astype(jnp.bfloat16)
        if seen == rows:
            sum_k[...] = add_k
            sum_v[...] = add_v
        else:
            sum_k[0:seen, :] += add_k
            sum_v[0:seen, :] += add_v
    gk_ref[...] = sum_k[...].astype(jnp.bfloat16)
    gv_ref[...] = sum_v[...].astype(jnp.bfloat16)


def attend(qkv, segments):
    rows, width = qkv.shape[0], qkv.shape[1] // 3
    pairs = width // 128
    return pl.pallas_call(
        functools.partial(attend_kernel, HEADS),
        grid=(pairs,),
        in_specs=[
            pl.BlockSpec((1, rows), lambda i: (0, 0)),
            pl.BlockSpec((rows, 1), lambda i: (0, 0)),
            pl.BlockSpec((rows, 128), lambda i: (0, i)),
            pl.BlockSpec((rows, 128), lambda i: (0, i + pairs)),
            pl.BlockSpec((rows, 128), lambda i: (0, i + 2 * pairs)),
        ],
        out_specs=[
            pl.BlockSpec((rows, 128), lambda i: (0, i)),
            pl.BlockSpec((1, 2, rows), lambda i: (i, 0, 0)),
        ],
        out_shape=[
            jax.ShapeDtypeStruct((rows, width), jnp.bfloat16),
            jax.ShapeDtypeStruct((pairs, 2, rows), jnp.float32),
        ],
        scratch_shapes=[pltpu.VMEM((rows, rows), jnp.float32)],
        compiler_params=pltpu.CompilerParams(vmem_limit_bytes=40 * MIB),
        name="attend",
    )(segments, segments.reshape(rows, 1), qkv, qkv, qkv)


def attend_back(qkv, segments, grad_mixed, lse):
    rows, width = grad_mixed.shape
    pairs = width // 128
    block = pl.BlockSpec((rows, 128), lambda i: (0, i))
    return pl.pallas_call(
        functools.partial(attend_back_kernel, HEADS),
        grid=(pairs,),
        in_specs=[
            pl.BlockSpec((1, rows), lambda i: (0, 0)),
            pl.BlockSpec((rows, 1), lambda i: (0, 0)),
            block,
            pl.BlockSpec((rows, 128), lambda i: (0, i + pairs)),
            pl.BlockSpec((rows, 128), lambda i: (0, i + 2 * pairs)),
            block,
            pl.BlockSpec((1, 2, rows), lambda i: (i, 0, 0)),
        ],
        out_specs=[block, block, block],
        out_shape=[jax.ShapeDtypeStruct((rows, width), jnp.bfloat16)] * 3,
        scratch_shapes=[
            pltpu.VMEM((rows, rows), jnp.float32),
            pltpu.VMEM((rows, 128), jnp.float32),
            pltpu.VMEM((rows, 128), jnp.float32),
        ],
        compiler_params=pltpu.CompilerParams(vmem_limit_bytes=40 * MIB),
        name="attend_back",
    )(segments, segments.reshape(rows, 1), qkv, qkv, qkv, grad_mixed, lse)


def pack(pieces, shape):
    joined = jnp.concatenate([p.astype(jnp.bfloat16) for p in pieces], axis=-1)
    room = shape[-2] * shape[-1] - joined.shape[-1]
    pad = [(0, 0)] * (joined.ndim - 1) + [(0, room)]
    return jnp.pad(joined, pad).reshape((-1, shape[-1]))


def unpack(packed, count, sizes):
    flat = packed.reshape(count, -1)
    out, at = [], 0
    for size in sizes:
        out.append(flat[:, at : at + size].reshape(-1))
        at += size
    return out


def shards(
    tokens,
    segments,
    ln1_gain,
    ln1_bias,
    w_qkv,
    q_bias,
    v_bias,
    w_out,
    out_bias,
    ln2_gain,
    ln2_bias,
    w_up,
    up_bias,
    w_down,
    down_bias,
    cotangent,
):
    count = lax.axis_size("shard")
    vectors = (
        ln1_gain,
        ln1_bias,
        q_bias,
        v_bias,
        out_bias,
        ln2_gain,
        ln2_bias,
        down_bias,
        up_bias,
    )
    sizes = [v.shape[0] for v in vectors]
    small_rows = -(-sum(sizes) // (256 * 128)) * 128
    small = (small_rows, 256)
    small_full, qkv_matrix, out_matrix, up_matrix, down_matrix = gather_all(
        count, [pack(vectors, small), w_qkv, w_out, w_up, w_down]
    )
    (
        first_gain,
        first_shift,
        query_bias,
        value_bias,
        out_shift,
        second_gain,
        second_shift,
        down_shift,
        up_shift,
    ) = unpack(small_full, count, sizes)
    rows, width = tokens.shape
    inputs = by_rows(tokens.astype(jnp.float32))
    normed_one, scale_one = normalize(inputs)
    first = (normed_one * first_gain.astype(jnp.float32) + first_shift.astype(jnp.float32)).astype(
        jnp.bfloat16
    )
    joined = jnp.concatenate([query_bias, jnp.zeros_like(query_bias), value_bias]).astype(
        jnp.float32
    )
    first = by_rows(first)
    qkv = (jnp.dot(first, qkv_matrix, preferred_element_type=jnp.float32) + joined).astype(
        jnp.bfloat16
    )
    mixed, lse = attend(qkv, segments)
    middle = (
        inputs
        + jnp.dot(mixed, out_matrix, preferred_element_type=jnp.float32)
        + out_shift.astype(jnp.float32)
    )
    middle = by_rows(middle)
    normed_two, scale_two = normalize(middle)
    second = (
        normed_two * second_gain.astype(jnp.float32) + second_shift.astype(jnp.float32)
    ).astype(jnp.bfloat16)
    second = by_rows(second)
    upper = jnp.dot(second, up_matrix, preferred_element_type=jnp.float32) + up_shift.astype(
        jnp.float32
    )
    tanh_value = jnp.tanh(GELU_C * (upper + GELU_A * upper * upper * upper))
    active = (0.5 * upper * (1.0 + tanh_value)).astype(jnp.bfloat16)
    output = (
        middle
        + jnp.dot(active, down_matrix, preferred_element_type=jnp.float32)
        + down_shift.astype(jnp.float32)
    ).astype(jnp.bfloat16)
    down_shift_grad = column_sum(cotangent)
    down_grad = left_dot(active, cotangent)
    grad_active = right_dot(cotangent, down_matrix)
    gelu_slope = 0.5 * (1.0 + tanh_value) + 0.5 * upper * (
        1.0 - tanh_value * tanh_value
    ) * GELU_C * (1.0 + 3.0 * GELU_A * upper * upper)
    grad_upper = (grad_active * gelu_slope).astype(jnp.bfloat16)
    up_shift_grad = column_sum(grad_upper)
    up_grad = left_dot(second, grad_upper)
    grad_second = by_rows(right_dot(grad_upper, up_matrix))
    second_gain_grad = jnp.sum(grad_second * normed_two, axis=0)
    second_shift_grad = jnp.sum(grad_second, axis=0)
    grad_middle = cotangent.astype(jnp.float32) + norm_back(
        grad_second, normed_two, scale_two, second_gain.astype(jnp.float32)
    )
    grad_middle = by_rows(grad_middle)
    grad_branch = grad_middle.astype(jnp.bfloat16)
    out_shift_grad = column_sum(grad_branch)
    out_grad = left_dot(mixed, grad_branch)
    grad_mixed = right_dot(grad_branch, out_matrix).astype(jnp.bfloat16)
    grad_qkv = jnp.concatenate(attend_back(qkv, segments, grad_mixed, lse), axis=1)
    query_bias_grad = column_sum(grad_qkv[:, :width])
    value_bias_grad = column_sum(grad_qkv[:, 2 * width :])
    qkv_grad = left_dot(first, grad_qkv)
    grad_first = by_rows(right_dot(grad_qkv, qkv_matrix))
    first_gain_grad = jnp.sum(grad_first * normed_one, axis=0)
    first_shift_grad = jnp.sum(grad_first, axis=0)
    token_grad = (
        grad_middle + norm_back(grad_first, normed_one, scale_one, first_gain.astype(jnp.float32))
    ).astype(jnp.bfloat16)
    grads = (
        first_gain_grad,
        first_shift_grad,
        query_bias_grad,
        value_bias_grad,
        out_shift_grad,
        second_gain_grad,
        second_shift_grad,
        down_shift_grad,
        up_shift_grad,
    )
    packed = pack([g.reshape(count, -1) for g in grads], small)
    shares = reduce_all(
        count,
        [
            down_grad.astype(jnp.bfloat16),
            up_grad.astype(jnp.bfloat16),
            out_grad.astype(jnp.bfloat16),
            qkv_grad.astype(jnp.bfloat16),
            packed,
        ],
    )
    shares = [share.astype(jnp.float32) for share in shares]
    groups = lax.axis_size("rep") // GROUP
    if groups > 1:
        shares = [share / GROUP for share in lax.psum(shares, "rep")]
    down_sum, up_sum, out_sum, qkv_sum, small_sum = shares
    (
        ln1_gain_sum,
        ln1_bias_sum,
        q_bias_sum,
        v_bias_sum,
        out_bias_sum,
        ln2_gain_sum,
        ln2_bias_sum,
        down_bias_sum,
        up_bias_sum,
    ) = unpack(small_sum, 1, sizes)
    return (
        output,
        token_grad,
        ln1_gain_sum,
        ln1_bias_sum,
        qkv_sum,
        q_bias_sum,
        v_bias_sum,
        out_sum,
        out_bias_sum,
        ln2_gain_sum,
        ln2_bias_sum,
        up_sum,
        up_bias_sum,
        down_sum,
        down_bias_sum,
    )


def solution(mesh):
    in_specs = (
        P(("rep", "shard"), None),
        P(("rep", "shard"), None),
        P("shard"),
        P("shard"),
        P("shard", None),
        P("shard"),
        P("shard"),
        P("shard", None),
        P("shard"),
        P("shard"),
        P("shard"),
        P("shard", None),
        P("shard"),
        P("shard", None),
        P("shard"),
        P(("rep", "shard"), None),
    )
    out_specs = (
        P(("rep", "shard"), None),
        P(("rep", "shard"), None),
        P("shard"),
        P("shard"),
        P("shard", None),
        P("shard"),
        P("shard"),
        P("shard", None),
        P("shard"),
        P("shard"),
        P("shard"),
        P("shard", None),
        P("shard"),
        P("shard", None),
        P("shard"),
    )
    return jax.shard_map(shards, mesh=mesh, in_specs=in_specs, out_specs=out_specs, check_vma=False)
```
